1024 devices in a mesh: group: 32 (over x, y, core), member: 32 (over z).
Axes of the slice: x: 4, y: 4, z: 32, core: 2. Of those that a mesh axis runs over, the one named last changes fastest.
Arguments:
- rows: bfloat16 [262144, 1024], P(('group', 'member')), may hold values from -9 to 9
- top_ids: int32 [262144], P(('group', 'member')), may hold values from 0 to 4095, as said below
- border_ids: int32 [4096], P(('group', 'member')), may hold values from 0 to 4095, as said below
- centroids: bfloat16 [4096, 64, 1024], P(('group', 'member')), may hold values from -6 to 6
- mass: float32 [4096, 64], P(('group', 'member')), may hold values from 1 to 64
Outputs:
- refined: float32 [4096, 64, 1024], P(('group', 'member'))
- new_mass: float32 [4096, 64], P(('group', 'member'))
The draws below stay inside these ranges and needn't reach their ends.
Inputs may be any that keep to these rules, and one draw needn't show every extreme that they name: `top_ids`: top cluster c lives on device c // 4 (devices numbered group-major, member index (c // 4) % 32). Every device holds exactly 8 rows whose top cluster lies on each member index. The rows held by the 32 devices of one group whose top cluster lies on one given device number at most 16; for every member index some device reaches that bound from every group, so it receives 512 rows. `border_ids`: the border cluster of a top cluster differs from it and lies on the same device or on the device with the next member index in the same group; on the device with the last member index it lies on the same device.
All inputs are finite; a program needn't handle non-finite values.
Results may differ from the reference program's by a relative error of at most 0.0037.
Values may be sent and summed in bfloat16 or wider, within the bound.
A program may use at most 32 MiB of HBM per device.

```python
import math
import jax
import jax.numpy as jnp
from jax import lax

D = 1024
SUB = 64
CLU_DEV = 4
ITERS = 2
TOK_DEV = 256
CLUSTERS = 4096
TOKENS = 262144
SLOTS = 512
N_GROUP = 32
N_MEMBER = 32


def shuffle_order(key, shape):
    noise = jax.random.randint(key, shape, 0, 2 ** 20)
    score = noise * 1024 + jnp.arange(shape[-1], dtype=jnp.int32)
    return jnp.argsort(score, axis=-1, stable=True)


def route_table(key):
    key = jax.random.fold_in(key, 101)
    keys = jax.random.split(key, 6)
    per_member = TOK_DEV // N_MEMBER
    capacity = 2 * TOK_DEV // N_GROUP
    tickets = N_GROUP * capacity
    popular = jax.random.randint(keys[0], (N_MEMBER, N_GROUP), 1, 9)
    jitter = jax.random.randint(keys[1], (N_GROUP, N_MEMBER, N_GROUP), 0, 3)
    forced = jax.random.randint(keys[2], (N_MEMBER,), 0, N_GROUP)
    ticket = jnp.arange(capacity, dtype=jnp.int32)
    weight = popular[None, :, :] + jitter
    primary = ((ticket + 1) * 64)[None, None, None, :] // weight[:, :, :, None] + 1
    index = jnp.arange(N_GROUP, dtype=jnp.int32)[:, None] * capacity + ticket[None, :]
    score = primary * tickets + index[None, None, :, :]
    favoured = jnp.arange(N_GROUP, dtype=jnp.int32)[None, None, :, None] == forced[None, :, None, None]
    score = jnp.where(favoured, index[None, None, :, :], score).reshape(N_GROUP, N_MEMBER, tickets)
    chosen = jnp.argsort(score, axis=-1, stable=True)[:, :, :TOK_DEV]
    dest_group = (chosen // capacity).astype(jnp.int32)
    mixing = shuffle_order(keys[3], (N_GROUP, N_MEMBER, TOK_DEV))
    dest_group = jnp.take_along_axis(dest_group, mixing, axis=-1)
    dest_group = dest_group.reshape(N_GROUP, N_MEMBER, N_MEMBER, per_member).transpose(0, 2, 1, 3)
    local = jax.random.randint(keys[4], (N_GROUP, N_MEMBER, N_MEMBER, per_member), 0, CLU_DEV)
    member_ids = jnp.arange(N_MEMBER, dtype=jnp.int32)[None, None, :, None]
    top = ((dest_group * N_MEMBER + member_ids) * CLU_DEV + local).reshape(N_GROUP, N_MEMBER, TOK_DEV)
    placing = shuffle_order(keys[5], (N_GROUP, N_MEMBER, TOK_DEV))
    top = jnp.take_along_axis(top, placing, axis=-1)
    return top.reshape(TOKENS).astype(jnp.int32)


def centroid_table(key):
    key = jax.random.fold_in(key, 202)
    first = jax.random.fold_in(key, 0)
    normal = jax.random.truncated_normal(first, -6.0, 6.0, (CLUSTERS, SUB, D), jnp.float32)
    base = normal
    twin = base[:, 1]
    return base.at[:, 1].set(twin)


def draw_top_ids(key, part):
    return route_table(key)


def draw_centroids(key, part):
    return centroid_table(key).astype(jnp.bfloat16)


def draw_rows(key, part):
    key = jax.random.fold_in(key, 7)
    return jax.random.truncated_normal(key, -6.0, 6.0, (TOKENS, D), jnp.float32).astype(jnp.bfloat16)


def draw_border_ids(key, part):
    key = jax.random.fold_in(key, 5)
    cluster = jnp.arange(CLUSTERS, dtype=jnp.int32)
    device = cluster // CLU_DEV
    local = cluster % CLU_DEV
    last = device % N_MEMBER == N_MEMBER - 1
    reach = jnp.where(last, CLU_DEV - 1, 2 * CLU_DEV - 1)
    pick = jax.random.randint(key, (CLUSTERS,), 0, 2 ** 20) % reach
    offset = pick + (pick >= local).astype(jnp.int32)
    return (device * CLU_DEV + offset).astype(jnp.int32)


def block_scale(rng, extent, cuts, smallest, top_value):
    level = 1.0
    for axis_at, shards_of in cuts:
        draws = jax.random.uniform(jax.random.fold_in(jax.random.fold_in(rng, 6), axis_at), (shards_of,), jnp.float32, smallest / len(cuts), top_value / len(cuts))
        level = level * jnp.repeat(jnp.exp(draws), extent[axis_at] // shards_of).reshape((-1,) + (1,) * (len(extent) - 1 - axis_at))
    return level


def setup_inputs(seed: int = 0) -> dict:
    seeds = jax.random.split(jax.random.key(seed), 6)
    return {
        "rows": draw_rows(jax.random.fold_in(seeds[5], 71), 0),
        "top_ids": draw_top_ids(jax.random.fold_in(seeds[5], 71), 0),
        "border_ids": draw_border_ids(jax.random.fold_in(seeds[5], 71), 0),
        "centroids": draw_centroids(jax.random.fold_in(seeds[5], 71), 0),
        "mass": jnp.clip(jnp.exp(math.log(64.0) - 4.158883 * jax.random.uniform(seeds[4], (CLUSTERS, SUB), jnp.float32) ** block_scale(seeds[4], (CLUSTERS, SUB), ((0, 1024),), -0.2, 0.2)), 1.0, 64.0),
    }


SOFTMAX_HEAT = 32.0
PRIOR = 4.0
BALANCE = 1.0
KEEP = 0.5


def owner_terms(position_rows, slot_local, own_c, border_c, own_bias, border_bias):
    width = own_c.shape[-1]
    member_count = position_rows.shape[0]
    home_flattened = own_c.reshape(CLU_DEV * SUB, width)
    boundary_flattened = border_c.reshape(CLU_DEV * SUB, width)
    home_squared_norm = jnp.sum(jnp.square(home_flattened.astype(jnp.float32)), axis=1)
    boundary_squared_norm = jnp.sum(jnp.square(boundary_flattened.astype(jnp.float32)), axis=1)
    home_logit_value = (2.0 * jnp.dot(position_rows, home_flattened.T, preferred_element_type=jnp.float32) - home_squared_norm) / SOFTMAX_HEAT
    home_logit_value = home_logit_value - own_bias.reshape(-1).astype(jnp.float32)
    boundary_logit_value = (2.0 * jnp.dot(position_rows, boundary_flattened.T, preferred_element_type=jnp.float32) - boundary_squared_norm) / SOFTMAX_HEAT
    boundary_logit_value = boundary_logit_value - border_bias.reshape(-1).astype(jnp.float32)
    mask = slot_local[:, None] == jnp.arange(CLU_DEV, dtype=jnp.int32)[None, :]
    own_sel = jnp.sum(jnp.where(mask[:, :, None], home_logit_value.reshape(member_count, CLU_DEV, SUB), 0.0), axis=1)
    border_sel = jnp.sum(jnp.where(mask[:, :, None], boundary_logit_value.reshape(member_count, CLU_DEV, SUB), 0.0), axis=1)
    joined = jnp.concatenate([own_sel, border_sel], axis=1)
    top = jnp.max(joined, axis=1, keepdims=True)
    expo = jnp.exp(joined - top)
    valid = slot_local >= 0
    weight = jnp.where(valid[:, None], expo / jnp.sum(expo, axis=1, keepdims=True), 0.0).astype(jnp.bfloat16)
    weight = weight.astype(jnp.float32)
    own_spread = jnp.where(mask[:, :, None], weight[:, None, :SUB], 0.0)
    border_spread = jnp.where(mask[:, :, None], weight[:, None, SUB:], 0.0)
    rows_f = position_rows.astype(jnp.float32)
    own_tot = jnp.einsum("rks,rd->ksd", own_spread, rows_f, precision=lax.Precision.HIGHEST)
    border_tot = jnp.einsum("rks,rd->ksd", border_spread, rows_f, precision=lax.Precision.HIGHEST)
    return own_tot, border_tot, jnp.sum(own_spread, axis=0), jnp.sum(border_spread, axis=0)


def owner_step(parts):
    return owner_terms(parts[0], parts[1], parts[2], parts[3], parts[4], parts[5])


def reference(rows, top_ids, border_ids, centroids, mass):
    owners = N_GROUP * N_MEMBER
    owner = (top_ids // CLU_DEV).astype(jnp.int32)
    order = jnp.argsort(owner, stable=True).astype(jnp.int32)
    sorted_owner = owner[order]
    start = jnp.searchsorted(sorted_owner, jnp.arange(owners, dtype=jnp.int32)).astype(jnp.int32)
    rank = jnp.arange(TOKENS, dtype=jnp.int32) - start[sorted_owner]
    place = (sorted_owner * SLOTS + rank).astype(jnp.int32)
    position_rows = jnp.zeros((owners * SLOTS, D), jnp.bfloat16).at[place].set(rows[order]).reshape(owners, SLOTS, D)
    slot_local = jnp.full((owners * SLOTS,), -1, jnp.int32).at[place].set((top_ids[order] % CLU_DEV).astype(jnp.int32))
    slot_local = slot_local.reshape(owners, SLOTS)
    state = centroids.astype(jnp.float32)
    mass_now = mass
    scoring = centroids
    for step in range(ITERS):
        bias = (BALANCE * jnp.log(mass_now)).astype(jnp.bfloat16)
        own_c = scoring.reshape(owners, CLU_DEV, SUB, D)
        border_c = scoring[border_ids].reshape(owners, CLU_DEV, SUB, D)
        own_bias = bias.reshape(owners, CLU_DEV, SUB)
        border_bias = bias[border_ids].reshape(owners, CLU_DEV, SUB)
        own_tot, border_tot, own_cnt, border_cnt = lax.map(owner_step, (position_rows, slot_local, own_c, border_c, own_bias, border_bias))
        sums = own_tot.reshape(CLUSTERS, SUB, D).at[border_ids].add(border_tot.reshape(CLUSTERS, SUB, D))
        counts = own_cnt.reshape(CLUSTERS, SUB).at[border_ids].add(border_cnt.reshape(CLUSTERS, SUB))
        state = (PRIOR * state + sums) / (PRIOR + counts)[:, :, None]
        mass_now = KEEP * mass_now + counts
        scoring = state.astype(jnp.bfloat16)
    return state, mass_now
```

```python
import functools

import jax
import jax.numpy as jnp
from jax import lax
from jax.experimental import pallas as pl
from jax.experimental.pallas import tpu as pltpu
from jax.sharding import PartitionSpec as P

ITERS = 2
SOFTMAX_HEAT = 32.0
PRIOR = 4.0
BALANCE = 1.0
KEEP = 0.5

CHUNKS = 2
LANES = 128
LOW = -1e30
MESH = pl.DeviceIdType.MESH
F32, BF16, I32 = jnp.float32, jnp.bfloat16, jnp.int32


def log2(n):
    assert n & (n - 1) == 0
    return n.bit_length() - 1


def iota(shape, dim):
    return lax.broadcasted_iota(I32, shape, dim)


def onehot(cond):
    return jnp.where(cond, 1.0, 0.0).astype(BF16)


def dot(a, b):
    return jnp.dot(a, b, preferred_element_type=F32)


def dot_t(a, b):
    return lax.dot_general(a, b, (((1,), (1,)), ((), ())), preferred_element_type=F32)


def lane_row(row, matrix):
    many = jnp.broadcast_to(row.astype(F32), (16, row.shape[1])).astype(BF16)
    return dot_t(many, matrix)[0:1].astype(I32)


def ranked(label, classes):
    n = label.shape[1]
    hit = iota((classes, n), 0) == label
    before = dot(onehot(hit), onehot(iota((n, n), 0) < iota((n, n), 1)))
    return jnp.sum(jnp.where(hit, before, 0.0), axis=0, keepdims=True).astype(I32)


def kernel(
    M, G,
    rows_ref, ids_ref, border_ref, cent_ref, mass_ref,
    out_ref, mass_out_ref,
    rsend, ra, rb, gsx, gsy, x, y,
    idmsg, ida, idb, locmsg, locx, ymsg, yrecv, st_send, st_recv,
    ids_s, ids_r, idf_s, idf_r, row_s, row_r, fwd_s, fwd_r,
    loc_s, loc_r, grp_s, grp_r, y_s, y_r, st_s, st_r,
):
    tok, D = rows_ref.shape
    C, SUB = mass_ref.shape
    K = C * SUB
    pm = tok // M
    slab = 2 * pm
    half = M // 2
    cap = 2 * tok // G
    slots = G * cap
    W = D // CHUNKS
    H = W // 2
    g = lax.axis_index("group")
    m = lax.axis_index("member")
    right = {"member": (m + 1) % M}
    left = {"member": (m + M - 1) % M}

    def remote(src, dst, ssem, rsem, dev):
        return pltpu.make_async_remote_copy(
            src_ref=src, dst_ref=dst, send_sem=ssem, recv_sem=rsem,
            device_id=dev, device_id_type=MESH)

    def wait(ref, sem):
        pltpu.make_async_copy(ref, ref, sem).wait()

    barrier = pltpu.get_barrier_semaphore()

    @pl.loop(1, M)
    def _(d):
        pl.semaphore_signal(barrier, inc=1, device_id={"member": (m + d) % M}, device_id_type=MESH)

    @pl.loop(1, G)
    def _(j):
        pl.semaphore_signal(barrier, inc=1, device_id={"group": (g + j) % G}, device_id_type=MESH)

    ids = ids_ref[...]
    rel = (((ids >> log2(C)) & (M - 1)) - m) & (M - 1)
    slot = rel * pm + ranked(rel, M)
    coded = ((ids >> log2(C * M)) << log2(C)) | (ids & (C - 1))
    ordered = lane_row(coded, onehot(iota((tok, tok), 0) == slot))
    per = LANES // pm
    for b in range(tok // LANES):
        part = ordered[:, b * LANES:(b + 1) * LANES].reshape(1, 1, LANES)
        keep = iota((per, 1, LANES), 2) >> log2(pm) == iota((per, 1, LANES), 0)
        idmsg[b * per:(b + 1) * per] = jnp.where(keep, part, 0)
    q = iota((2 * tok, tok), 0)
    same = ((q >> log2(slab)) * pm + (q & (pm - 1))) == slot
    second = ((q >> log2(pm)) & 1) == 1
    pick0 = onehot(same & ~second)
    pick1 = onehot(same & second)

    def order_rows(c):
        rsend[c] = (dot(pick0, rows_ref[:, c * W:c * W + H])
                    + dot(pick1, rows_ref[:, c * W + H:(c + 1) * W])).astype(BF16)

    order_rows(0)
    pl.semaphore_wait(barrier, M - 1 + G - 1)

    @pl.loop(1, half)
    def _(d):
        remote(idmsg.at[d], ida.at[d], ids_s.at[0], ids_r.at[0], {"member": (m + d) % M}).start()
        e = M - 1 - d
        remote(idmsg.at[e], idb.at[e], ids_s.at[1], ids_r.at[1], {"member": (m + M - d) % M}).start()

    ida[0] = idmsg[0]
    idb[M - 1] = idmsg[M - 1]

    def at(d):
        return pl.ds(pl.multiple_of(d * slab, slab), slab)

    def send_rows(c):
        @pl.loop(1, half)
        def _(d):
            e = M - 1 - d
            remote(rsend.at[c, at(d)], ra.at[c, at(d)], row_s.at[c, 0], row_r.at[c, 0],
                   {"member": (m + d) % M}).start()
            remote(rsend.at[c, at(e)], rb.at[c, at(e)], row_s.at[c, 1], row_r.at[c, 1],
                   {"member": (m + M - d) % M}).start()
        ra[c, 0:slab] = rsend[c, 0:slab]
        rb[c, (M - 1) * slab:] = rsend[c, (M - 1) * slab:]

    send_rows(0)
    for c in range(1, CHUNKS):
        order_rows(c)
        send_rows(c)

    wait(ida.at[1:half], ids_r.at[0])
    remote(ida.at[0:half], idb.at[0:half], idf_s.at[0], idf_r.at[0], right).start()
    wait(idb.at[half:M - 1], ids_r.at[1])
    remote(idb.at[half:M], ida.at[half:M], idf_s.at[1], idf_r.at[1], left).start()
    wait(ida.at[half:M], idf_r.at[1])
    wait(idb.at[0:half], idf_r.at[0])

    def group_place(ref):
        code = jnp.concatenate(
            [jnp.sum(ref[b * per:(b + 1) * per], axis=0) for b in range(tok // LANES)], axis=1)
        toward = ((code >> log2(C)) - g) & (G - 1)
        rank = ranked(toward, G)
        return code, toward, rank

    def group_picks(toward, rank):
        wide = iota((2 * tok, tok), 0)
        spread = onehot(((wide >> log2(slab)) * pm + (wide & (pm - 1))) == iota((2 * tok, tok), 1))
        place = lane_row(toward, spread) * cap + lane_row(rank, spread)
        fits = iota((slots, 2 * tok), 0) == place
        upper = ((iota((slots, 2 * tok), 1) >> log2(pm)) & 1) == 1
        return onehot(fits & ~upper), onehot(fits & upper)

    code, toward, rank = group_place(ida)
    local1 = lane_row((code & (C - 1)) + 1, onehot(iota((slots, tok), 0) == toward * cap + rank))
    pj = max(LANES // cap, 1)
    span = max(LANES, cap)
    for b in range(slots // span):
        part = local1[:, b * span:(b + 1) * span].reshape(1, 1, span)
        keep = iota((pj, 1, span), 2) >> log2(cap) == iota((pj, 1, span), 0)
        locmsg[b * pj:(b + 1) * pj] = jnp.where(keep, part, 0)

    @pl.loop(1, G)
    def _(j):
        remote(locmsg.at[j], locx.at[j], loc_s, loc_r, {"group": (g + j) % G}).start()

    locx[0] = locmsg[0]
    xp = group_picks(toward, rank)
    _, toward_b, rank_b = group_place(idb)
    yp = group_picks(toward_b, rank_b)

    wait(locx.at[1:G], loc_r)
    local = jnp.concatenate(
        [jnp.sum(locx[b * pj:(b + 1) * pj], axis=0) for b in range(slots // span)], axis=1) - 1
    base = (g * M + m) * C
    edge = jnp.full((1, slots), -1, I32)
    for k in range(C):
        edge = jnp.where(local == k, border_ref[:, k:k + 1] - base, edge)
    ymsg[...] = jnp.where(local >= 0, edge - C, -1)
    remote(ymsg, yrecv, y_s, y_r, right).start()

    def gat(j):
        return pl.ds(pl.multiple_of(j * cap, cap), cap)

    def forward(c):
        wait(ra.at[c, slab:half * slab], row_r.at[c, 0])
        remote(ra.at[c, 0:half * slab], rb.at[c, 0:half * slab],
               fwd_s.at[c, 0], fwd_r.at[c, 0], right).start()
        wait(rb.at[c, half * slab:(M - 1) * slab], row_r.at[c, 1])
        remote(rb.at[c, half * slab:], ra.at[c, half * slab:],
               fwd_s.at[c, 1], fwd_r.at[c, 1], left).start()

    def regroup(c, which):
        pool, send, land, picks = ((ra, gsx, x, xp), (rb, gsy, y, yp))[which]
        if which == 0:
            wait(ra.at[c, half * slab:], fwd_r.at[c, 1])
        else:
            wait(rb.at[c, 0:half * slab], fwd_r.at[c, 0])
        have = pool[c]
        for h in range(2):
            send[c, :, h * H:(h + 1) * H] = dot(picks[h], have).astype(BF16)

        @pl.loop(1, G)
        def _(j):
            remote(send.at[c, gat(j)], land.at[c, gat(j)], grp_s.at[c, which], grp_r.at[c, which],
                   {"group": (g + j) % G}).start()
        land[c, 0:cap] = send[c, 0:cap]

    for c in range(CHUNKS):
        forward(c)
        regroup(c, 0)
        regroup(c, 1)

    eye = iota((SUB, SUB), 0) == iota((SUB, SUB), 1)

    def to_column(table):
        return jnp.concatenate(
            [jnp.sum(jnp.where(eye, table[k:k + 1], 0.0), axis=1, keepdims=True)
             for k in range(C)], axis=0)

    block = iota((K, 1), 0) >> log2(SUB)
    wait(yrecv, y_r)
    mask_x = (block == local) | (block == edge)
    mask_y = block == yrecv[...]
    mass_now = to_column(mass_ref[...])
    for step in range(ITERS):
        bias = (BALANCE * jnp.log(mass_now)).astype(BF16).astype(F32)
        if step == 0:
            scoring = cent_ref
            state = cent_ref[...].astype(F32)
        else:
            scoring = out_ref[...].astype(BF16)
            state = out_ref[...]
        norm = jnp.sum(jnp.square(scoring[...].astype(F32)), axis=1, keepdims=True)
        lx = jnp.zeros((K, slots), F32)
        ly = jnp.zeros((K, slots), F32)
        for c in range(CHUNKS):
            part = scoring[:, c * W:(c + 1) * W]
            if step == 0:
                wait(x.at[c, cap:], grp_r.at[c, 0])
            lx = lx + dot_t(part, x[c])
            if step == 0:
                wait(y.at[c, cap:], grp_r.at[c, 1])
            ly = ly + dot_t(part, y[c])

        def local_terms(product, mask, slot_at):
            logit = jnp.where(mask, (2.0 * product - norm) / SOFTMAX_HEAT - bias, LOW)
            top = jnp.max(logit, axis=0, keepdims=True)
            expo = jnp.where(mask, jnp.exp(logit - top), 0.0)
            total = jnp.sum(expo, axis=0, keepdims=True)
            st_send[slot_at, :, 0:slots] = top
            st_send[slot_at, :, slots:] = total
            return expo, top, total

        ix, iy = 2 * step, 2 * step + 1
        ex, tx, sx = local_terms(lx, mask_x, ix)
        remote(st_send.at[ix], st_recv.at[ix], st_s.at[ix], st_r.at[ix], right).start()
        ey, ty, sy = local_terms(ly, mask_y, iy)
        remote(st_send.at[iy], st_recv.at[iy], st_s.at[iy], st_r.at[iy], left).start()

        def weights(expo, top, total, slot_at):
            wait(st_recv.at[slot_at], st_r.at[slot_at])
            other_top = st_recv[slot_at, :, 0:slots]
            other_total = st_recv[slot_at, :, slots:]
            most = jnp.maximum(top, other_top)
            mine = jnp.exp(top - most)
            whole = total * mine + other_total * jnp.exp(other_top - most)
            return (expo * (mine / jnp.where(whole > 0.0, whole, 1.0))).astype(BF16)

        wx = weights(ex, tx, sx, iy)
        wy = weights(ey, ty, sy, ix)
        count = (jnp.sum(wx.astype(F32), axis=1, keepdims=True)
                 + jnp.sum(wy.astype(F32), axis=1, keepdims=True))
        scale = 1.0 / (PRIOR + count)
        for c in range(CHUNKS):
            cols = slice(c * W, (c + 1) * W)
            sums = dot(wx, x[c]) + dot(wy, y[c])
            out_ref[:, cols] = (PRIOR * state[:, cols] + sums) * scale
        mass_now = KEEP * mass_now + count
    for k in range(C):
        mass_out_ref[k:k + 1, :] = jnp.sum(
            jnp.where(eye, mass_now[k * SUB:(k + 1) * SUB], 0.0), axis=0, keepdims=True)

    wait(idmsg.at[1:half], ids_s.at[0])
    wait(idmsg.at[half:M - 1], ids_s.at[1])
    wait(ida.at[0:half], idf_s.at[0])
    wait(idb.at[half:M], idf_s.at[1])
    wait(locmsg.at[1:G], loc_s)
    wait(ymsg, y_s)
    for c in range(CHUNKS):
        wait(rsend.at[c, slab:half * slab], row_s.at[c, 0])
        wait(rsend.at[c, half * slab:(M - 1) * slab], row_s.at[c, 1])
        wait(ra.at[c, 0:half * slab], fwd_s.at[c, 0])
        wait(rb.at[c, half * slab:], fwd_s.at[c, 1])
        wait(gsx.at[c, cap:], grp_s.at[c, 0])
        wait(gsy.at[c, cap:], grp_s.at[c, 1])
    for i in range(2 * ITERS):
        wait(st_send.at[i], st_s.at[i])


def body(rows, top_ids, border_ids, centroids, mass):
    M = lax.axis_size("member")
    G = lax.axis_size("group")
    tok, D = rows.shape
    C, SUB = mass.shape
    cap = 2 * tok // G
    slots = G * cap
    W = D // CHUNKS
    span = max(LANES, cap)
    vmem = pl.BlockSpec(memory_space=pltpu.VMEM)
    dma = pltpu.SemaphoreType.DMA
    pool = pltpu.VMEM((CHUNKS, 2 * tok, W // 2), BF16)
    grouped = pltpu.VMEM((CHUNKS, slots, W), BF16)
    codes = pltpu.VMEM((M, 1, LANES), I32)
    locals_ = pltpu.VMEM((G, 1, span), I32)
    lane = pltpu.VMEM((1, slots), I32)
    stats = pltpu.VMEM((2 * ITERS, 1, 2 * slots), F32)
    refined, new_mass = pl.pallas_call(
        functools.partial(kernel, M, G),
        out_shape=(jax.ShapeDtypeStruct((C * SUB, D), F32), jax.ShapeDtypeStruct((C, SUB), F32)),
        in_specs=[vmem] * 5,
        out_specs=(vmem, vmem),
        scratch_shapes=[
            pool, pool, pool, grouped, grouped, grouped, grouped,
            codes, codes, codes, locals_, locals_, lane, lane, stats, stats,
            dma((2,)), dma((2,)), dma((2,)), dma((2,)),
            dma((CHUNKS, 2)), dma((CHUNKS, 2)), dma((CHUNKS, 2)), dma((CHUNKS, 2)),
            dma, dma, dma((CHUNKS, 2)), dma((CHUNKS, 2)), dma, dma,
            dma((2 * ITERS,)), dma((2 * ITERS,)),
        ],
        compiler_params=pltpu.CompilerParams(
            collective_id=0, has_side_effects=True, vmem_limit_bytes=48 * 1024 * 1024),
    )(rows, top_ids.reshape(1, tok), border_ids.reshape(1, C),
      centroids.reshape(C * SUB, D), mass)
    return refined.reshape(C, SUB, D), new_mass


def solution(mesh):
    in_specs = (
        P(("group", "member"), None),
        P(("group", "member")),
        P(("group", "member")),
        P(("group", "member"), None, None),
        P(("group", "member"), None),
    )
    out_specs = (P(("group", "member"), None, None), P(("group", "member"), None))
    return jax.shard_map(body, mesh=mesh, in_specs=in_specs, out_specs=out_specs, check_vma=False)
```

```python
import functools

import jax
import jax.numpy as jnp
from jax import lax
from jax.experimental import pallas as pl
from jax.experimental.pallas import tpu as pltpu
from jax.sharding import PartitionSpec as P

ITERS = 2
SOFTMAX_HEAT = 32.0
PRIOR = 4.0
BALANCE = 1.0
KEEP = 0.5

CHUNKS = 4
NEAR = 7
LANES = 128
LOW = -1e30
MESH = pl.DeviceIdType.MESH
F32, BF16, I32 = jnp.float32, jnp.bfloat16, jnp.int32


def log2(n):
    assert n & (n - 1) == 0
    return n.bit_length() - 1


def iota(shape, dim):
    return lax.broadcasted_iota(I32, shape, dim)


def onehot(cond):
    return jnp.where(cond, 1.0, 0.0).astype(BF16)


def dot(a, b):
    return jnp.dot(a, b, preferred_element_type=F32)


def dot_t(a, b):
    return lax.dot_general(a, b, (((1,), (1,)), ((), ())), preferred_element_type=F32)


def lane_row(row, matrix):
    many = jnp.broadcast_to(row.astype(F32), (16, row.shape[1])).astype(BF16)
    return dot_t(many, matrix)[0:1].astype(I32)


def ranked(label, classes):
    n = label.shape[1]
    hit = iota((classes, n), 0) == label
    before = dot(onehot(hit), onehot(iota((n, n), 0) < iota((n, n), 1)))
    return jnp.sum(jnp.where(hit, before, 0.0), axis=0, keepdims=True).astype(I32)


def kernel(
    M, G,
    rows_hbm, ids_ref, border_ref, cent_hbm, mass_ref,
    out_ref, mass_out_ref,
    rows_ref, cent_ref, rsend, ra, rb, gsx, gsy, x, y,
    idmsg, ida, idb, locmsg, locx, ymsg, yrecv, st_send, st_recv,
    ids_s, ids_r, idf_s, idf_r, row_s, row_r, fwd_s, fwd_r,
    loc_s, loc_r, grp_s, grp_r, y_s, y_r, st_s, st_r, in_sem,
):
    tok, D = rows_hbm.shape
    C, SUB = mass_ref.shape
    K = C * SUB
    pm = tok // M
    slab = 2 * pm
    half = M // 2
    near = min(NEAR, half - 1)
    cap = 2 * tok // G
    slots = G * cap
    W = D // CHUNKS
    H = W // 2
    g = lax.axis_index("group")
    m = lax.axis_index("member")
    right = {"member": (m + 1) & (M - 1)}
    left = {"member": (m + M - 1) & (M - 1)}

    def remote(src, dst, ssem, rsem, dev):
        return pltpu.make_async_remote_copy(
            src_ref=src, dst_ref=dst, send_sem=ssem, recv_sem=rsem,
            device_id=dev, device_id_type=MESH)

    def wait(ref, sem):
        pltpu.make_async_copy(ref, ref, sem).wait()

    barrier = pltpu.get_barrier_semaphore()

    @pl.loop(1, M)
    def _(d):
        pl.semaphore_signal(barrier, inc=1, device_id={"member": (m + d) & (M - 1)}, device_id_type=MESH)

    @pl.loop(1, G)
    def _(j):
        pl.semaphore_signal(barrier, inc=1, device_id={"group": (g + j) & (G - 1)}, device_id_type=MESH)

    rows_in = pltpu.make_async_copy(rows_hbm, rows_ref, in_sem.at[0])
    cent_in = pltpu.make_async_copy(cent_hbm, cent_ref, in_sem.at[1])
    rows_in.start()
    cent_in.start()

    ids = ids_ref[...]
    rel = (((ids >> log2(C)) & (M - 1)) - m) & (M - 1)
    slot = rel * pm + ranked(rel, M)
    coded = ((ids >> log2(C * M)) << log2(C)) | (ids & (C - 1))
    ordered = lane_row(coded, onehot(iota((tok, tok), 0) == slot))
    per = LANES // pm
    for b in range(tok // LANES):
        part = ordered[:, b * LANES:(b + 1) * LANES].reshape(1, 1, LANES)
        keep = iota((per, 1, LANES), 2) >> log2(pm) == iota((per, 1, LANES), 0)
        idmsg[b * per:(b + 1) * per] = jnp.where(keep, part, 0)
    q = iota((2 * tok, tok), 0)
    same = ((q >> log2(slab)) * pm + (q & (pm - 1))) == slot
    second = ((q >> log2(pm)) & 1) == 1
    pick0 = onehot(same & ~second)
    pick1 = onehot(same & second)

    def order_rows(c):
        rsend[c] = (dot(pick0, rows_ref[:, c * W:c * W + H])
                    + dot(pick1, rows_ref[:, c * W + H:(c + 1) * W])).astype(BF16)

    rows_in.wait()
    order_rows(0)
    pl.semaphore_wait(barrier, M - 1 + G - 1)

    @pl.loop(1, half)
    def _(d):
        remote(idmsg.at[d], ida.at[d], ids_s.at[0], ids_r.at[0], {"member": (m + d) & (M - 1)}).start()
        e = M - 1 - d
        remote(idmsg.at[e], idb.at[e], ids_s.at[1], ids_r.at[1], {"member": (m + M - d) & (M - 1)}).start()

    ida[0] = idmsg[0]
    idb[M - 1] = idmsg[M - 1]

    def at(d):
        return pl.ds(pl.multiple_of(d * slab, slab), slab)

    def send_rows(c):
        for first, last, which in ((1, near, 0), (near, half, 1)):
            @pl.loop(first, last)
            def _(d):
                e = M - 1 - d
                remote(rsend.at[c, at(d)], ra.at[c, at(d)], row_s.at[c, 0], row_r.at[c, which],
                       {"member": (m + d) & (M - 1)}).start()
                remote(rsend.at[c, at(e)], rb.at[c, at(e)], row_s.at[c, 1], row_r.at[c, 2 + which],
                       {"member": (m + M - d) & (M - 1)}).start()

        ra[c, 0:slab] = rsend[c, 0:slab]
        rb[c, (M - 1) * slab:] = rsend[c, (M - 1) * slab:]

    send_rows(0)
    for c in range(1, CHUNKS):
        order_rows(c)

    wait(ida.at[1:half], ids_r.at[0])
    remote(ida.at[0:half], idb.at[0:half], idf_s.at[0], idf_r.at[0], right).start()
    wait(idb.at[half:M - 1], ids_r.at[1])
    remote(idb.at[half:M], ida.at[half:M], idf_s.at[1], idf_r.at[1], left).start()
    wait(ida.at[half:M], idf_r.at[1])
    wait(idb.at[0:half], idf_r.at[0])
    if CHUNKS > 1:
        send_rows(1)

    def group_place(ref):
        code = jnp.concatenate(
            [jnp.sum(ref[b * per:(b + 1) * per], axis=0) for b in range(tok // LANES)], axis=1)
        toward = ((code >> log2(C)) - g) & (G - 1)
        rank = ranked(toward, G)
        return code, toward, rank

    def group_picks(toward, rank):
        wide = iota((2 * tok, tok), 0)
        spread = onehot(((wide >> log2(slab)) * pm + (wide & (pm - 1))) == iota((2 * tok, tok), 1))
        place = lane_row(toward, spread) * cap + lane_row(rank, spread)
        fits = iota((slots, 2 * tok), 0) == place
        upper = ((iota((slots, 2 * tok), 1) >> log2(pm)) & 1) == 1
        return onehot(fits & ~upper), onehot(fits & upper)

    code, toward, rank = group_place(ida)
    local1 = lane_row((code & (C - 1)) + 1, onehot(iota((slots, tok), 0) == toward * cap + rank))
    pj = max(LANES // cap, 1)
    span = max(LANES, cap)
    for b in range(slots // span):
        part = local1[:, b * span:(b + 1) * span].reshape(1, 1, span)
        keep = iota((pj, 1, span), 2) >> log2(cap) == iota((pj, 1, span), 0)
        locmsg[b * pj:(b + 1) * pj] = jnp.where(keep, part, 0)

    @pl.loop(1, G)
    def _(j):
        remote(locmsg.at[j], locx.at[j], loc_s, loc_r, {"group": (g + j) & (G - 1)}).start()

    locx[0] = locmsg[0]
    xp = group_picks(toward, rank)
    _, toward_b, rank_b = group_place(idb)
    yp = group_picks(toward_b, rank_b)

    def share_local():
        wait(locx.at[1:G], loc_r)
        local = jnp.concatenate(
            [jnp.sum(locx[b * pj:(b + 1) * pj], axis=0) for b in range(slots // span)], axis=1) - 1
        base = (g * M + m) * C
        edge = jnp.full((1, slots), -1, I32)
        for k in range(C):
            edge = jnp.where(local == k, border_ref[:, k:k + 1] - base, edge)
        ymsg[...] = jnp.where(local >= 0, edge - C, -1)
        remote(ymsg, yrecv, y_s, y_r, right).start()
        return local, edge

    def gat(j):
        return pl.ds(pl.multiple_of(j * cap, cap), cap)

    def wait_near(c):
        wait(ra.at[c, slab:near * slab], row_r.at[c, 0])
        wait(rb.at[c, (M - near) * slab:(M - 1) * slab], row_r.at[c, 2])

    def forward(c):
        wait(ra.at[c, near * slab:half * slab], row_r.at[c, 1])
        remote(ra.at[c, 0:half * slab], rb.at[c, 0:half * slab],
               fwd_s.at[c, 0], fwd_r.at[c, 0], right).start()
        wait(rb.at[c, half * slab:(M - near) * slab], row_r.at[c, 3])
        remote(rb.at[c, half * slab:], ra.at[c, half * slab:],
               fwd_s.at[c, 1], fwd_r.at[c, 1], left).start()

    def regroup(c, which):
        pool, send, land, picks = ((ra, gsx, x, xp), (rb, gsy, y, yp))[which]
        if which == 0:
            wait(ra.at[c, half * slab:], fwd_r.at[c, 1])
        else:
            wait(rb.at[c, 0:half * slab], fwd_r.at[c, 0])
        have = pool[c]
        for h in range(2):
            send[c, :, h * H:(h + 1) * H] = dot(picks[h], have).astype(BF16)

        @pl.loop(1, G)
        def _(j):
            remote(send.at[c, gat(j)], land.at[c, gat(j)], grp_s.at[c, which], grp_r.at[c, which],
                   {"group": (g + j) & (G - 1)}).start()
        land[c, 0:cap] = send[c, 0:cap]

    wait_near(0)
    for c in range(CHUNKS):
        forward(c)
        if c + 1 < CHUNKS:
            wait_near(c + 1)
        if c + 2 < CHUNKS:
            send_rows(c + 2)
        regroup(c, 0)
        regroup(c, 1)
        if c == 0:
            local, edge = share_local()

    eye = iota((SUB, SUB), 0) == iota((SUB, SUB), 1)

    def to_column(table):
        return jnp.concatenate(
            [jnp.sum(jnp.where(eye, table[k:k + 1], 0.0), axis=1, keepdims=True)
             for k in range(C)], axis=0)

    block = iota((K, 1), 0) >> log2(SUB)
    wait(yrecv, y_r)
    mask_x = (block == local) | (block == edge)
    mask_y = block == yrecv[...]
    mass_now = to_column(mass_ref[...])
    cent_in.wait()
    for step in range(ITERS):
        bias = (BALANCE * jnp.log(mass_now)).astype(BF16).astype(F32)
        if step == 0:
            scoring = cent_ref
            state = cent_ref[...].astype(F32)
        else:
            scoring = out_ref[...].astype(BF16)
            state = out_ref[...]
        norm = jnp.sum(jnp.square(scoring[...].astype(F32)), axis=1, keepdims=True)
        lx = jnp.zeros((K, slots), F32)
        ly = jnp.zeros((K, slots), F32)
        for c in range(CHUNKS):
            part = scoring[:, c * W:(c + 1) * W]
            if step == 0:
                wait(x.at[c, cap:], grp_r.at[c, 0])
            lx = lx + dot_t(part, x[c])
            if step == 0:
                wait(y.at[c, cap:], grp_r.at[c, 1])
            ly = ly + dot_t(part, y[c])

        def local_terms(product, mask, slot_at):
            logit = jnp.where(mask, (2.0 * product - norm) / SOFTMAX_HEAT - bias, LOW)
            top = jnp.max(logit, axis=0, keepdims=True)
            expo = jnp.where(mask, jnp.exp(logit - top), 0.0)
            total = jnp.sum(expo, axis=0, keepdims=True)
            st_send[slot_at, :, 0:slots] = top
            st_send[slot_at, :, slots:] = total
            return expo, top, total

        ix, iy = 2 * step, 2 * step + 1
        ex, tx, sx = local_terms(lx, mask_x, ix)
        remote(st_send.at[ix], st_recv.at[ix], st_s.at[ix], st_r.at[ix], right).start()
        ey, ty, sy = local_terms(ly, mask_y, iy)
        remote(st_send.at[iy], st_recv.at[iy], st_s.at[iy], st_r.at[iy], left).start()

        def weights(expo, top, total, slot_at):
            wait(st_recv.at[slot_at], st_r.at[slot_at])
            other_top = st_recv[slot_at, :, 0:slots]
            other_total = st_recv[slot_at, :, slots:]
            most = jnp.maximum(top, other_top)
            mine = jnp.exp(top - most)
            whole = total * mine + other_total * jnp.exp(other_top - most)
            return (expo * (mine / jnp.where(whole > 0.0, whole, 1.0))).astype(BF16)

        wx = weights(ex, tx, sx, iy)
        wy = weights(ey, ty, sy, ix)
        count = (jnp.sum(wx.astype(F32), axis=1, keepdims=True)
                 + jnp.sum(wy.astype(F32), axis=1, keepdims=True))
        scale = 1.0 / (PRIOR + count)
        for c in range(CHUNKS):
            cols = slice(c * W, (c + 1) * W)
            sums = dot(wx, x[c]) + dot(wy, y[c])
            out_ref[:, cols] = (PRIOR * state[:, cols] + sums) * scale
        mass_now = KEEP * mass_now + count
    for k in range(C):
        mass_out_ref[k:k + 1, :] = jnp.sum(
            jnp.where(eye, mass_now[k * SUB:(k + 1) * SUB], 0.0), axis=0, keepdims=True)

    wait(idmsg.at[1:half], ids_s.at[0])
    wait(idmsg.at[half:M - 1], ids_s.at[1])
    wait(ida.at[0:half], idf_s.at[0])
    wait(idb.at[half:M], idf_s.at[1])
    wait(locmsg.at[1:G], loc_s)
    wait(ymsg, y_s)
    for c in range(CHUNKS):
        wait(rsend.at[c, slab:half * slab], row_s.at[c, 0])
        wait(rsend.at[c, half * slab:(M - 1) * slab], row_s.at[c, 1])
        wait(ra.at[c, 0:half * slab], fwd_s.at[c, 0])
        wait(rb.at[c, half * slab:], fwd_s.at[c, 1])
        wait(gsx.at[c, cap:], grp_s.at[c, 0])
        wait(gsy.at[c, cap:], grp_s.at[c, 1])
    for i in range(2 * ITERS):
        wait(st_send.at[i], st_s.at[i])


def body(rows, top_ids, border_ids, centroids, mass):
    M = lax.axis_size("member")
    G = lax.axis_size("group")
    tok, D = rows.shape
    C, SUB = mass.shape
    cap = 2 * tok // G
    slots = G * cap
    W = D // CHUNKS
    span = max(LANES, cap)
    vmem = pl.BlockSpec(memory_space=pltpu.VMEM)
    anywhere = pl.BlockSpec(memory_space=pl.ANY)
    dma = pltpu.SemaphoreType.DMA
    pool = pltpu.VMEM((CHUNKS, 2 * tok, W // 2), BF16)
    grouped = pltpu.VMEM((CHUNKS, slots, W), BF16)
    codes = pltpu.VMEM((M, 1, LANES), I32)
    locals_ = pltpu.VMEM((G, 1, span), I32)
    lane = pltpu.VMEM((1, slots), I32)
    stats = pltpu.VMEM((2 * ITERS, 1, 2 * slots), F32)
    refined, new_mass = pl.pallas_call(
        functools.partial(kernel, M, G),
        out_shape=(jax.ShapeDtypeStruct((C * SUB, D), F32), jax.ShapeDtypeStruct((C, SUB), F32)),
        in_specs=[anywhere, vmem, vmem, anywhere, vmem],
        out_specs=(vmem, vmem),
        scratch_shapes=[
            pltpu.VMEM((tok, D), BF16), pltpu.VMEM((C * SUB, D), BF16), pool, pool, pool, grouped, grouped, grouped, grouped,
            codes, codes, codes, locals_, locals_, lane, lane, stats, stats,
            dma((2,)), dma((2,)), dma((2,)), dma((2,)),
            dma((CHUNKS, 2)), dma((CHUNKS, 4)), dma((CHUNKS, 2)), dma((CHUNKS, 2)),
            dma, dma, dma((CHUNKS, 2)), dma((CHUNKS, 2)), dma, dma,
            dma((2 * ITERS,)), dma((2 * ITERS,)), dma((2,)),
        ],
        compiler_params=pltpu.CompilerParams(
            collective_id=0, has_side_effects=True, vmem_limit_bytes=56 * 1024 * 1024),
    )(rows, top_ids.reshape(1, tok), border_ids.reshape(1, C),
      centroids.reshape(C * SUB, D), mass)
    return refined.reshape(C, SUB, D), new_mass


def solution(mesh):
    in_specs = (
        P(("group", "member"), None),
        P(("group", "member")),
        P(("group", "member")),
        P(("group", "member"), None, None),
        P(("group", "member"), None),
    )
    out_specs = (P(("group", "member"), None, None), P(("group", "member"), None))
    return jax.shard_map(body, mesh=mesh, in_specs=in_specs, out_specs=out_specs, check_vma=False)
```

```python
import functools

import jax
import jax.numpy as jnp
from jax import lax
from jax.experimental import pallas as pl
from jax.experimental.pallas import tpu as pltpu
from jax.sharding import PartitionSpec as P

ITERS = 2
SOFTMAX_HEAT = 32.0
PRIOR = 4.0
BALANCE = 1.0
KEEP = 0.5

CHUNKS = 4
NEAR = 7
LANES = 128
LOW = -1e30
MESH = pl.DeviceIdType.MESH
F32, BF16, I32 = jnp.float32, jnp.bfloat16, jnp.int32


def log2(n):
    assert n & (n - 1) == 0
    return n.bit_length() - 1


def iota(shape, dim):
    return lax.broadcasted_iota(I32, shape, dim)


def onehot(cond):
    return jnp.where(cond, 1.0, 0.0).astype(BF16)


def dot(a, b):
    return jnp.dot(a, b, preferred_element_type=F32)


def dot_t(a, b):
    return lax.dot_general(a, b, (((1,), (1,)), ((), ())), preferred_element_type=F32)


def lane_row(row, matrix):
    many = jnp.broadcast_to(row.astype(F32), (16, row.shape[1])).astype(BF16)
    return dot_t(many, matrix)[0:1].astype(I32)


def ranked(label, classes):
    n = label.shape[1]
    hit = iota((classes, n), 0) == label
    before = dot(onehot(hit), onehot(iota((n, n), 0) < iota((n, n), 1)))
    return jnp.sum(jnp.where(hit, before, 0.0), axis=0, keepdims=True).astype(I32)


def kernel(
    M, G,
    rows_hbm, ids_ref, border_ref, cent_hbm, mass_ref,
    out_ref, mass_out_ref,
    rows_ref, cent_ref, rsend, ra, rb, gsx, gsy, x, y,
    idmsg, ida, idb, locmsg, locx, ymsg, yrecv, st_send, st_recv,
    ids_s, ids_r, idf_s, idf_r, row_s, row_r, fwd_s, fwd_r,
    loc_s, loc_r, grp_s, grp_r, y_s, y_r, st_s, st_r, in_sem,
):
    tok, D = rows_hbm.shape
    C, SUB = mass_ref.shape
    K = C * SUB
    pm = tok // M
    slab = 2 * pm
    half = M // 2
    near = min(NEAR, half - 1)
    cap = 2 * tok // G
    slots = G * cap
    W = D // CHUNKS
    H = W // 2
    g = lax.axis_index("group")
    m = lax.axis_index("member")
    right = {"member": (m + 1) & (M - 1)}
    left = {"member": (m + M - 1) & (M - 1)}

    def remote(src, dst, ssem, rsem, dev):
        return pltpu.make_async_remote_copy(
            src_ref=src, dst_ref=dst, send_sem=ssem, recv_sem=rsem,
            device_id=dev, device_id_type=MESH)

    def wait(ref, sem):
        pltpu.make_async_copy(ref, ref, sem).wait()

    rows_in = pltpu.make_async_copy(rows_hbm, rows_ref, in_sem.at[0])
    cent_in = pltpu.make_async_copy(cent_hbm, cent_ref, in_sem.at[1])
    rows_in.start()
    cent_in.start()

    barrier = pltpu.get_barrier_semaphore()

    @pl.loop(1, M)
    def _(d):
        pl.semaphore_signal(barrier, inc=1, device_id={"member": (m + d) & (M - 1)}, device_id_type=MESH)

    @pl.loop(1, G)
    def _(j):
        pl.semaphore_signal(barrier, inc=1, device_id={"group": (g + j) & (G - 1)}, device_id_type=MESH)

    ids = ids_ref[...]
    rel = (((ids >> log2(C)) & (M - 1)) - m) & (M - 1)
    slot = rel * pm + ranked(rel, M)
    coded = ((ids >> log2(C * M)) << log2(C)) | (ids & (C - 1))
    ordered = lane_row(coded, onehot(iota((tok, tok), 0) == slot))
    per = LANES // pm
    for b in range(tok // LANES):
        part = ordered[:, b * LANES:(b + 1) * LANES].reshape(1, 1, LANES)
        keep = iota((per, 1, LANES), 2) >> log2(pm) == iota((per, 1, LANES), 0)
        idmsg[b * per:(b + 1) * per] = jnp.where(keep, part, 0)
    q = iota((2 * tok, tok), 0)
    same = ((q >> log2(slab)) * pm + (q & (pm - 1))) == slot
    second = ((q >> log2(pm)) & 1) == 1
    pick0 = onehot(same & ~second)
    pick1 = onehot(same & second)

    def order_rows(c):
        rsend[c] = (dot(pick0, rows_ref[:, c * W:c * W + H])
                    + dot(pick1, rows_ref[:, c * W + H:(c + 1) * W])).astype(BF16)

    rows_in.wait()
    order_rows(0)
    pl.semaphore_wait(barrier, M - 1 + G - 1)

    @pl.loop(1, half)
    def _(d):
        remote(idmsg.at[d], ida.at[d], ids_s.at[0], ids_r.at[0], {"member": (m + d) & (M - 1)}).start()
        e = M - 1 - d
        remote(idmsg.at[e], idb.at[e], ids_s.at[1], ids_r.at[1], {"member": (m + M - d) & (M - 1)}).start()

    ida[0] = idmsg[0]
    idb[M - 1] = idmsg[M - 1]

    def at(d):
        return pl.ds(pl.multiple_of(d * slab, slab), slab)

    def send_rows(c):
        for first, last, which in ((1, near, 0), (near, half, 1)):
            @pl.loop(first, last)
            def _(d):
                e = M - 1 - d
                remote(rsend.at[c, at(d)], ra.at[c, at(d)], row_s.at[c, 0], row_r.at[c, which],
                       {"member": (m + d) & (M - 1)}).start()
                remote(rsend.at[c, at(e)], rb.at[c, at(e)], row_s.at[c, 1], row_r.at[c, 2 + which],
                       {"member": (m + M - d) & (M - 1)}).start()

        ra[c, 0:slab] = rsend[c, 0:slab]
        rb[c, (M - 1) * slab:] = rsend[c, (M - 1) * slab:]

    send_rows(0)
    for c in range(1, CHUNKS):
        order_rows(c)
        if c == 1:
            send_rows(c)

    wait(ida.at[1:half], ids_r.at[0])
    remote(ida.at[0:half], idb.at[0:half], idf_s.at[0], idf_r.at[0], right).start()
    wait(idb.at[half:M - 1], ids_r.at[1])
    remote(idb.at[half:M], ida.at[half:M], idf_s.at[1], idf_r.at[1], left).start()
    wait(ida.at[half:M], idf_r.at[1])
    wait(idb.at[0:half], idf_r.at[0])

    def group_place(ref):
        code = jnp.concatenate(
            [jnp.sum(ref[b * per:(b + 1) * per], axis=0) for b in range(tok // LANES)], axis=1)
        toward = ((code >> log2(C)) - g) & (G - 1)
        rank = ranked(toward, G)
        return code, toward, rank

    def group_picks(toward, rank):
        wide = iota((2 * tok, tok), 0)
        spread = onehot(((wide >> log2(slab)) * pm + (wide & (pm - 1))) == iota((2 * tok, tok), 1))
        place = lane_row(toward, spread) * cap + lane_row(rank, spread)
        fits = iota((slots, 2 * tok), 0) == place
        upper = ((iota((slots, 2 * tok), 1) >> log2(pm)) & 1) == 1
        return onehot(fits & ~upper), onehot(fits & upper)

    code, toward, rank = group_place(ida)
    local1 = lane_row((code & (C - 1)) + 1, onehot(iota((slots, tok), 0) == toward * cap + rank))
    pj = max(LANES // cap, 1)
    span = max(LANES, cap)
    for b in range(slots // span):
        part = local1[:, b * span:(b + 1) * span].reshape(1, 1, span)
        keep = iota((pj, 1, span), 2) >> log2(cap) == iota((pj, 1, span), 0)
        locmsg[b * pj:(b + 1) * pj] = jnp.where(keep, part, 0)

    @pl.loop(1, G)
    def _(j):
        remote(locmsg.at[j], locx.at[j], loc_s, loc_r, {"group": (g + j) & (G - 1)}).start()

    locx[0] = locmsg[0]
    xp = group_picks(toward, rank)
    _, toward_b, rank_b = group_place(idb)
    yp = group_picks(toward_b, rank_b)

    def share_local():
        wait(locx.at[1:G], loc_r)
        local = jnp.concatenate(
            [jnp.sum(locx[b * pj:(b + 1) * pj], axis=0) for b in range(slots // span)], axis=1) - 1
        base = (g * M + m) * C
        edge = jnp.full((1, slots), -1, I32)
        for k in range(C):
            edge = jnp.where(local == k, border_ref[:, k:k + 1] - base, edge)
        ymsg[...] = jnp.where(local >= 0, edge - C, -1)
        remote(ymsg, yrecv, y_s, y_r, right).start()
        return local, edge

    def gat(j):
        return pl.ds(pl.multiple_of(j * cap, cap), cap)

    def wait_near(c):
        wait(ra.at[c, slab:near * slab], row_r.at[c, 0])
        remote(ra.at[c, 0:near * slab], rb.at[c, 0:near * slab],
               fwd_s.at[c, 0], fwd_r.at[c, 0], right).start()
        wait(rb.at[c, (M - near) * slab:(M - 1) * slab], row_r.at[c, 2])
        remote(rb.at[c, (M - near) * slab:], ra.at[c, (M - near) * slab:],
               fwd_s.at[c, 1], fwd_r.at[c, 1], left).start()

    def forward(c):
        wait(ra.at[c, near * slab:half * slab], row_r.at[c, 1])
        remote(ra.at[c, near * slab:half * slab], rb.at[c, near * slab:half * slab],
               fwd_s.at[c, 0], fwd_r.at[c, 0], right).start()
        wait(rb.at[c, half * slab:(M - near) * slab], row_r.at[c, 3])
        remote(rb.at[c, half * slab:(M - near) * slab], ra.at[c, half * slab:(M - near) * slab],
               fwd_s.at[c, 1], fwd_r.at[c, 1], left).start()

    def regroup(c, which):
        pool, send, land, picks = ((ra, gsx, x, xp), (rb, gsy, y, yp))[which]
        if which == 0:
            wait(ra.at[c, half * slab:], fwd_r.at[c, 1])
        else:
            wait(rb.at[c, 0:half * slab], fwd_r.at[c, 0])
        have = pool[c]
        for h in range(2):
            send[c, :, h * H:(h + 1) * H] = dot(picks[h], have).astype(BF16)

        @pl.loop(1, G)
        def _(j):
            remote(send.at[c, gat(j)], land.at[c, gat(j)], grp_s.at[c, which], grp_r.at[c, which],
                   {"group": (g + j) & (G - 1)}).start()
        land[c, 0:cap] = send[c, 0:cap]

    wait_near(0)
    for c in range(CHUNKS):
        forward(c)
        if c + 1 < CHUNKS:
            wait_near(c + 1)
        if c + 2 < CHUNKS:
            send_rows(c + 2)
        regroup(c, 0)
        regroup(c, 1)
        if c == 0:
            local, edge = share_local()

    eye = iota((SUB, SUB), 0) == iota((SUB, SUB), 1)

    def to_column(table):
        return jnp.concatenate(
            [jnp.sum(jnp.where(eye, table[k:k + 1], 0.0), axis=1, keepdims=True)
             for k in range(C)], axis=0)

    block = iota((K, 1), 0) >> log2(SUB)
    wait(yrecv, y_r)
    mask_x = (block == local) | (block == edge)
    mask_y = block == yrecv[...]
    mass_now = to_column(mass_ref[...])
    cent_in.wait()
    for step in range(ITERS):
        bias = (BALANCE * jnp.log(mass_now)).astype(BF16).astype(F32)
        if step == 0:
            scoring = cent_ref
            state = cent_ref[...].astype(F32)
        else:
            scoring = out_ref[...].astype(BF16)
            state = out_ref[...]
        norm = jnp.sum(jnp.square(scoring[...].astype(F32)), axis=1, keepdims=True)
        shift = norm * (1.0 / SOFTMAX_HEAT) + bias
        lx = jnp.zeros((K, slots), F32)
        ly = jnp.zeros((K, slots), F32)
        for c in range(CHUNKS):
            part = scoring[:, c * W:(c + 1) * W]
            if step == 0:
                wait(x.at[c, cap:], grp_r.at[c, 0])
            lx = lx + dot_t(part, x[c])
            if step == 0:
                wait(y.at[c, cap:], grp_r.at[c, 1])
            ly = ly + dot_t(part, y[c])

        def local_terms(product, mask, slot_at):
            logit = jnp.where(mask, product * (2.0 / SOFTMAX_HEAT) - shift, LOW)
            top = jnp.max(logit, axis=0, keepdims=True)
            expo = jnp.where(mask, jnp.exp(logit - top), 0.0)
            total = jnp.sum(expo, axis=0, keepdims=True)
            st_send[slot_at, :, 0:slots] = top
            st_send[slot_at, :, slots:] = total
            return expo, top, total

        ix, iy = 2 * step, 2 * step + 1
        ex, tx, sx = local_terms(lx, mask_x, ix)
        remote(st_send.at[ix], st_recv.at[ix], st_s.at[ix], st_r.at[ix], right).start()
        ey, ty, sy = local_terms(ly, mask_y, iy)
        remote(st_send.at[iy], st_recv.at[iy], st_s.at[iy], st_r.at[iy], left).start()

        def weights(expo, top, total, slot_at):
            wait(st_recv.at[slot_at], st_r.at[slot_at])
            other_top = st_recv[slot_at, :, 0:slots]
            other_total = st_recv[slot_at, :, slots:]
            most = jnp.maximum(top, other_top)
            mine = jnp.exp(top - most)
            whole = total * mine + other_total * jnp.exp(other_top - most)
            return (expo * (mine / jnp.where(whole > 0.0, whole, 1.0))).astype(BF16)

        wx = weights(ex, tx, sx, iy)
        wy = weights(ey, ty, sy, ix)
        count = (jnp.sum(wx.astype(F32), axis=1, keepdims=True)
                 + jnp.sum(wy.astype(F32), axis=1, keepdims=True))
        scale = 1.0 / (PRIOR + count)
        for c in range(CHUNKS):
            cols = slice(c * W, (c + 1) * W)
            sums = dot(wx, x[c]) + dot(wy, y[c])
            out_ref[:, cols] = (PRIOR * state[:, cols] + sums) * scale
        mass_now = KEEP * mass_now + count
    for k in range(C):
        mass_out_ref[k:k + 1, :] = jnp.sum(
            jnp.where(eye, mass_now[k * SUB:(k + 1) * SUB], 0.0), axis=0, keepdims=True)

    wait(idmsg.at[1:half], ids_s.at[0])
    wait(idmsg.at[half:M - 1], ids_s.at[1])
    wait(ida.at[0:half], idf_s.at[0])
    wait(idb.at[half:M], idf_s.at[1])
    wait(locmsg.at[1:G], loc_s)
    wait(ymsg, y_s)
    for c in range(CHUNKS):
        wait(rsend.at[c, slab:half * slab], row_s.at[c, 0])
        wait(rsend.at[c, half * slab:(M - 1) * slab], row_s.at[c, 1])
        wait(ra.at[c, 0:half * slab], fwd_s.at[c, 0])
        wait(rb.at[c, half * slab:], fwd_s.at[c, 1])
        wait(gsx.at[c, cap:], grp_s.at[c, 0])
        wait(gsy.at[c, cap:], grp_s.at[c, 1])
    for i in range(2 * ITERS):
        wait(st_send.at[i], st_s.at[i])


def body(rows, top_ids, border_ids, centroids, mass):
    M = lax.axis_size("member")
    G = lax.axis_size("group")
    tok, D = rows.shape
    C, SUB = mass.shape
    cap = 2 * tok // G
    slots = G * cap
    W = D // CHUNKS
    span = max(LANES, cap)
    vmem = pl.BlockSpec(memory_space=pltpu.VMEM)
    anywhere = pl.BlockSpec(memory_space=pl.ANY)
    dma = pltpu.SemaphoreType.DMA
    pool = pltpu.VMEM((CHUNKS, 2 * tok, W // 2), BF16)
    grouped = pltpu.VMEM((CHUNKS, slots, W), BF16)
    codes = pltpu.VMEM((M, 1, LANES), I32)
    locals_ = pltpu.VMEM((G, 1, span), I32)
    lane = pltpu.VMEM((1, slots), I32)
    stats = pltpu.VMEM((2 * ITERS, 1, 2 * slots), F32)
    refined, new_mass = pl.pallas_call(
        functools.partial(kernel, M, G),
        out_shape=(jax.ShapeDtypeStruct((C * SUB, D), F32), jax.ShapeDtypeStruct((C, SUB), F32)),
        in_specs=[anywhere, vmem, vmem, anywhere, vmem],
        out_specs=(vmem, vmem),
        scratch_shapes=[
            pltpu.VMEM((tok, D), BF16), pltpu.VMEM((C * SUB, D), BF16), pool, pool, pool, grouped, grouped, grouped, grouped,
            codes, codes, codes, locals_, locals_, lane, lane, stats, stats,
            dma((2,)), dma((2,)), dma((2,)), dma((2,)),
            dma((CHUNKS, 2)), dma((CHUNKS, 4)), dma((CHUNKS, 2)), dma((CHUNKS, 2)),
            dma, dma, dma((CHUNKS, 2)), dma((CHUNKS, 2)), dma, dma,
            dma((2 * ITERS,)), dma((2 * ITERS,)), dma((2,)),
        ],
        compiler_params=pltpu.CompilerParams(
            collective_id=0, has_side_effects=True, vmem_limit_bytes=56 * 1024 * 1024),
    )(rows, top_ids.reshape(1, tok), border_ids.reshape(1, C),
      centroids.reshape(C * SUB, D), mass)
    return refined.reshape(C, SUB, D), new_mass


def solution(mesh):
    in_specs = (
        P(("group", "member"), None),
        P(("group", "member")),
        P(("group", "member")),
        P(("group", "member"), None, None),
        P(("group", "member"), None),
    )
    out_specs = (P(("group", "member"), None, None), P(("group", "member"), None))
    return jax.shard_map(body, mesh=mesh, in_specs=in_specs, out_specs=out_specs, check_vma=False)
```
